256 devices in a mesh: expert: 16 (over z, core), token: 16 (over y, x).
Axes of the slice: x: 4, y: 4, z: 8, core: 2. Of those that a mesh axis runs over, the one named last changes fastest.
Arguments:
- tokens: bfloat16 [32768, 7168], P(('expert', 'token')), may hold values from -6 to 6
- routes: int32 [32768, 2], P(('expert', 'token')), may hold values from 0 to 15, all different within a row; in each aligned block of 128 rows (0 to 127, 128 to 255, ...) at most 32 rows name the same one
- owner_of: int32 [16], replicated, may hold values from 0 to 15, each once
- weights: bfloat16 [16, 2048, 7168], P('expert', 'token'), may hold values from -6 to 6
- hinv_diag: float32 [16, 128], P('expert'), may hold values from 0.5 to 2
- hinv_rows: float32 [16, 128, 7168], P('expert'), may hold values from -1 to 1
Outputs:
- gram: float32 [16, 7168, 128], P('expert', 'token')
- updated: bfloat16 [16, 2048, 7168], P('expert', 'token')
The draws below stay inside these ranges and needn't reach their ends.
Inputs may be any that keep to these rules, and one draw needn't show every extreme that they name: `routes`: among the tokens of one device (aligned blocks of 128 rows), no expert is named by more than 32 tokens, a bound that some block reaches; a token's experts are distinct. `owner_of`: each slot holds exactly one expert.
All inputs are finite; a program needn't handle non-finite values.
Results may differ from the reference program's by a relative error of at most 0.005.
Values may be sent and summed in bfloat16 or wider, within the bound.
A program may use at most 128 MiB of HBM per device.

```python
import math
import jax
import jax.numpy as jnp
import numpy as np
from jax import lax

D = 7168
FF = 2048
PANEL = 128
TOP = 2
TOK_DEV = 128
CAP = 32
EXPERTS = 16
TOKENS = 32768
N_EXPERT = 16
N_TOKEN = 16


def level_of(rng, extent, pieces, least, high):
    def one(dim, parts):
        heights = jax.random.uniform(jax.random.fold_in(jax.random.fold_in(rng, 6), dim), (parts,), jnp.float32, least / len(pieces), high / len(pieces))
        return jnp.repeat(jnp.exp(heights), extent[dim] // parts).reshape((-1,) + (1,) * (len(extent) - dim - 1))

    factor_of = one(*pieces[0])
    for cut in pieces[1:]:
        factor_of = factor_of * one(*cut)
    return factor_of


def shared_out(stream_key, own, number, rows, number_of, top, reach, slope):
    order = jax.random.permutation(stream_key, number_of)
    heavy_load, ordinary = load_shares(number_of, rows * top, reach, slope, True), load_shares(number_of, rows * top, reach, slope, False)
    places = jnp.arange(number_of)

    def named(lengths, turn):
        used = int((lengths > 0).sum())
        fixed = max(1, used // 4)
        passed = fixed + (places - fixed + turn * (used - fixed)) % max(1, number_of - fixed)
        return jnp.zeros((number_of,), jnp.int32).at[order[jnp.where(places < fixed, places, passed)]].set(jnp.asarray(lengths, jnp.int32))

    lengths = jnp.where(number % 4 == 0, named(heavy_load, number // 4), named(ordinary, number - number // 4 - 1))
    mixed = jax.random.permutation(jax.random.fold_in(own, 3), number_of)
    donor, sink = mixed[0:number_of // 2 * 2:2], mixed[1:number_of // 2 * 2:2]
    slack = jnp.minimum(lengths[donor] - 1, reach - lengths[sink]) // 2
    slack = jnp.where((donor == order[0]) | (sink == order[0]) | (lengths[sink] == 0), 0, jnp.maximum(slack, 0))
    passed = jax.random.randint(jax.random.fold_in(own, 4), (number_of // 2,), 0, 1 << 20) % (slack + 1)
    lengths = lengths.at[donor].add(-passed).at[sink].add(passed)
    labels = jnp.searchsorted(jnp.cumsum(lengths), jnp.arange(rows * top), side="right").astype(jnp.int32)
    listing = labels.reshape(top, rows).T
    listing = listing[jax.random.permutation(jax.random.fold_in(own, 1), rows)]
    turn = jax.random.randint(jax.random.fold_in(own, 2), (rows, 1), 0, top)
    return jnp.take_along_axis(listing, (jnp.arange(top)[None, :] + turn) % top, axis=1)


def load_shares(count, total, bound, skew, full):
    portions = [(1 << 20) // math.isqrt(standing ** skew) + 1 for standing in range(1, count + 1)]
    largest = bound if full else min(bound, max(-(-total // count), total * portions[0] // sum(portions)))
    least = 1 if total - largest >= count - 1 else 0
    given, surplus = [largest] + [least] * (count - 1), total - largest - least * (count - 1)
    while surplus > 0:
        movable = [i for i in range(1, count) if given[i] < largest] or [i for i in range(1, count) if given[i] < bound]
        mass, left = sum([portions[i] for i in movable]), surplus
        for i in movable:
            more = min(bound - given[i], max(1, left * portions[i] // mass), surplus)
            given[i] = given[i] + more
            surplus = surplus - more
    return np.array(given)


def scatter_about(key, extent, deviation, limit, split=(), held_as=jnp.bfloat16):
    array = jax.random.normal(key, extent, jnp.float32) * deviation
    if len(split) > 0:
        array = level_of(key, extent, split, -0.22, 0.18) * array
    return jnp.clip(array, min=-limit, max=limit).astype(held_as)


def setup_inputs(seed: int = 0) -> dict:
    streams_of = jax.random.split(jax.random.key(seed), 7)
    tokens = scatter_about(streams_of[0], (TOKENS, D), 1.0, 6.0, ((0, 256),))
    routes_keys = jax.random.split(jax.random.fold_in(streams_of[1], 1), TOKENS // TOK_DEV)
    routes_turns = jax.random.permutation(jax.random.fold_in(streams_of[1], 3), TOKENS // TOK_DEV)
    routes = jax.vmap(lambda own, number: shared_out(jax.random.fold_in(streams_of[1], 2), own, number, TOK_DEV, EXPERTS, TOP, CAP, 2))(routes_keys, routes_turns).reshape((TOKENS, TOP))
    owner_of = jax.random.permutation(streams_of[2], EXPERTS).astype(jnp.int32)
    weights = scatter_about(streams_of[3], (EXPERTS, FF, D), 1.0, 6.0, ((0, 16), (1, 16)))
    hinv_diag = jnp.clip(jnp.exp(math.log(2.0) - 1.3862944 * jax.random.uniform(streams_of[4], (EXPERTS, PANEL), jnp.float32) ** level_of(streams_of[4], (EXPERTS, PANEL), ((0, 16),), -0.2, 0.2)), 0.5, 2.0)
    hinv_rows = scatter_about(streams_of[5], (EXPERTS, PANEL, D), (PANEL // 4) ** -0.5, 1.0, ((0, 16),), jnp.float32)
    return dict(tokens=tokens, routes=routes, owner_of=owner_of, weights=weights, hinv_diag=hinv_diag, hinv_rows=hinv_rows)


def round_panel(weight_rows, colfac, diag_block, factor_rows):
    work = weight_rows.astype(jnp.float32)
    panel = work[:, :PANEL]
    step = lax.optimization_barrier(jnp.max(jnp.abs(panel), axis=1)) / 7.0 + 1e-06
    steps_grid = step[:, None] * colfac[None, :]
    column_ids = jnp.arange(PANEL)
    errors = jnp.zeros_like(panel)

    def advance(j, carry):
        panel, errors = carry
        value = lax.dynamic_slice_in_dim(panel, j, 1, 1)[:, 0]
        width = lax.dynamic_slice_in_dim(steps_grid, j, 1, 1)[:, 0]
        rounded = value - width / (2.0 * math.pi) * jnp.sin(2.0 * math.pi * value / width)
        fault = (value - rounded) / diag_block[j]
        row = lax.dynamic_slice_in_dim(factor_rows, j, 1, 0)[0, :PANEL]
        row = jnp.where(column_ids > j, row, 0.0)
        panel = panel - fault[:, None] * row[None, :]
        panel = jnp.where(column_ids[None, :] == j, rounded[:, None], panel)
        errors = jnp.where(column_ids[None, :] == j, fault[:, None], errors)
        return (panel, errors)
    panel, errors = lax.fori_loop(0, PANEL, advance, (panel, errors))
    rest = work[:, PANEL:] - jnp.dot(errors, factor_rows[:, PANEL:], precision=lax.Precision.HIGHEST)
    return jnp.concatenate([panel, rest], axis=1).astype(jnp.bfloat16)

def column_factors(gram_slot):
    dgram = jnp.diagonal(gram_slot[:PANEL, :])
    return jnp.sqrt(jnp.mean(dgram) / (dgram + 1e-05))

def reference(tokens, routes, owner_of, weights, hinv_diag, hinv_rows):
    scale = EXPERTS / (TOKENS * TOP)
    most_rows = N_EXPERT * N_TOKEN * CAP

    def expert_gram(expert):
        hit = jnp.any(routes == expert, axis=1)
        order = jnp.argsort(jnp.where(hit, 0, 1).astype(jnp.int32), stable=True)
        chosen = order[:most_rows]
        rows = jnp.where(hit[chosen][:, None], tokens[chosen], jnp.zeros((), jnp.bfloat16))
        return jnp.einsum('rd,rp->dp', rows, rows[:, :PANEL], preferred_element_type=jnp.float32) * scale
    by_expert = lax.map(expert_gram, jnp.arange(EXPERTS).astype(jnp.int32))
    gram = by_expert[jnp.argsort(owner_of).astype(jnp.int32)]

    def one_slot(slot):
        colfac = column_factors(gram[slot])
        return round_panel(weights[slot], colfac, hinv_diag[slot], hinv_rows[slot])
    updated = lax.map(one_slot, jnp.arange(EXPERTS).astype(jnp.int32))
    return (gram, updated)
```

```python
import math

import jax
import jax.numpy as jnp
from jax import lax
from jax.experimental import pallas as pl
from jax.experimental.pallas import tpu as pltpu
from jax.sharding import PartitionSpec as P

D = 7168
PANEL = 128
TOP = 2
TOK = 128
SLOTS = 16
RING = 8
PLANE = 16
SHARE = 448
MSG = PANEL + SLOTS
MESH = pl.DeviceIdType.MESH
BF16 = jnp.bfloat16
F32 = jnp.float32
SCALE = 16.0 / 65536.0

SINE = (
    6.2831852700170625,
    -16.20895564378196,
    16.769189671870134,
    -9.624604702175908,
    3.5163760294927235,
    -0.7983429889808796,
)


def sine_of_turns(turns):
    r = turns - jnp.round(turns)
    y = r * r
    y2 = y * y
    low = SINE[0] + SINE[1] * y
    mid = SINE[2] + SINE[3] * y
    top = SINE[4] + SINE[5] * y
    edge = r - 4.0 * (r * y)
    return edge * (low + y2 * (mid + y2 * top))


def place_of(x):
    return jnp.where(x == 0, 0, jnp.where(x == 3, 1, x + 1))


def kernel(
    tokens,
    routes,
    owner,
    weights,
    hdiag,
    hrows,
    gram,
    updated,
    x0,
    msg,
    w_v,
    h_v,
    out_v,
    dg_own,
    dg_in,
    dg_mid,
    dg_fin,
    mt,
    x_left,
    x_two,
    x_one,
    ht,
    rot,
    work,
    inv,
    amp,
    dinv,
    errs,
    sib_out,
    sib_in,
    own,
    z_out,
    z_in,
    fin,
    left,
    left_out,
    left_in,
    local_sem,
    dg_s,
    dg_r,
    dgz_s,
    dgz_r,
    pa_s,
    pa_r,
    pb_s,
    pb_r,
    xl_s,
    xl_r,
    x2_s,
    x2_r,
    x1_s,
    x1_r,
    sib_s,
    sib_r,
    z_s,
    z_r,
    lx_s,
    lx_r,
):
    e = lax.axis_index("expert")
    t = lax.axis_index("token")
    z, c = e // 2, e % 2
    y, x = t // 4, t % 4
    u = 4 * place_of(x) + y
    group = u // 8
    side = x % 2

    def plane_peer(k):
        py, px = (y + k // 4) % 4, (x + k % 4) % 4
        return py, px, 4 * place_of(px) + py

    def z_peer(i):
        dz = jnp.where(i % 2 == 1, 4 - (i + 1) // 2, 4 + i // 2)
        return (z + dz) % RING

    def main_lane(py, px):
        return pl.multiple_of((7 * (2 * py + px // 2) + 4 * (px % 2)) * 128, 128)

    def left_lane(py, m):
        return pl.multiple_of((7 * (2 * py + m) + 3) * 128, 128)

    def left_x(m):
        inner = jnp.where(group == 1, 1, 0)
        return jnp.where(m == 0, inner, 3 - inner)

    def remote(src, dst, send, recv, device):
        return pltpu.make_async_remote_copy(
            src_ref=src,
            dst_ref=dst,
            send_sem=send,
            recv_sem=recv,
            device_id=device,
            device_id_type=MESH,
        )

    barrier = pltpu.get_barrier_semaphore()

    @pl.loop(1, 16)
    def _(k):
        py, px, _ = plane_peer(k)
        pl.semaphore_signal(barrier, inc=1, device_id=(e, 4 * py + px), device_id_type=MESH)

    @pl.loop(1, 16)
    def _(k):
        pl.semaphore_signal(barrier, inc=1, device_id=((e + k) % 16, t), device_id_type=MESH)

    get_x0 = pltpu.make_async_copy(tokens.at[:, pl.ds(0, 128)], x0, local_sem.at[0])
    get_w = pltpu.make_async_copy(weights, w_v, local_sem.at[1])
    get_h = pltpu.make_async_copy(hrows, h_v, local_sem.at[2])
    get_x0.start()
    get_w.start()
    get_h.start()

    first = jnp.broadcast_to(routes[:, 0:1].astype(F32), (TOK, 128)).T[0:SLOTS].astype(jnp.int32)
    second = jnp.broadcast_to(routes[:, 1:2].astype(F32), (TOK, 128)).T[0:SLOTS].astype(jnp.int32)
    slot_a = jnp.zeros((SLOTS, 128), jnp.int32)
    slot_b = jnp.zeros((SLOTS, 128), jnp.int32)
    for i in range(SLOTS):
        slot_a = jnp.where(first == i, owner[i], slot_a)
        slot_b = jnp.where(second == i, owner[i], slot_b)
    slot_row = lax.broadcasted_iota(jnp.int32, (SLOTS, 128), 0)
    mask = jnp.where((slot_a == slot_row) | (slot_b == slot_row), 1.0, 0.0).astype(F32)

    get_x0.wait()
    panel = x0[...].astype(F32)
    square = panel * panel
    high = square.astype(BF16)
    low = (square - high.astype(F32)).astype(BF16)
    mask16 = mask.astype(BF16)
    dg_own[...] = jnp.dot(mask16, high, preferred_element_type=F32) + jnp.dot(
        mask16, low, preferred_element_type=F32
    )
    msg[pl.ds(u, 1), pl.ds(0, PANEL), :] = panel.T.astype(BF16)[None]
    msg[pl.ds(u, 1), pl.ds(PANEL, SLOTS), :] = mask16[None]

    pl.semaphore_wait(barrier, 30)

    @pl.loop(1, 16)
    def _(k):
        py, px, _ = plane_peer(k)
        remote(dg_own, dg_in.at[u], dg_s.at[k], dg_r.at[u], (e, 4 * py + px)).start()

    dg_in[pl.ds(u, 1)] = dg_own[...][None]

    @pl.loop(1, 4)
    def _(k):
        remote(msg.at[u], msg.at[u], pa_s.at[k], pa_r.at[y], (e, 4 * ((y + k) % 4) + x)).start()

    own_rows = pl.ds(pl.multiple_of(u * TOK, TOK), TOK)
    left_rows = pl.ds(pl.multiple_of((u - 8 * group) * TOK, TOK), TOK)

    @pl.loop(0, 8)
    def _(k):
        py, m = (y + k // 2) % 4, k % 2
        px = left_x(m)
        src = tokens.at[:, pl.ds(left_lane(py, m), 128)]
        itself = (py == y) & (px == x)

        @pl.when(jnp.logical_not(itself))
        def _():
            remote(src, x_left.at[left_rows], xl_s.at[k], xl_r.at[u - 8 * group], (e, 4 * py + px)).start()

        @pl.when(itself)
        def _():
            pltpu.make_async_copy(src, x_left.at[left_rows], local_sem.at[3]).start()

    keep_two = pltpu.make_async_copy(
        tokens.at[:, pl.ds(main_lane(y, x), 256)], x_two.at[own_rows], local_sem.at[4]
    )
    keep_one = pltpu.make_async_copy(
        tokens.at[:, pl.ds(main_lane(y, x) + 256, 128)], x_one.at[own_rows], local_sem.at[5]
    )
    keep_two.start()
    keep_one.start()

    @pl.loop(1, 4)
    def _(k):
        py = (y + k) % 4
        pu = 4 * (u // 4) + py
        remote(msg.at[pu], msg.at[pu], pa_s.at[k], pa_r.at[py], (e, 4 * py + x)).wait_recv()

    mine = pl.ds(4 * (u // 4), 4)

    @pl.loop(1, 4)
    def _(k):
        px = (x + k) % 4
        remote(msg.at[mine], msg.at[mine], pb_s.at[k], pb_r.at[x], (e, 4 * y + px)).start()

    @pl.loop(1, 16)
    def _(k):
        py, px, pu = plane_peer(k)
        src = tokens.at[:, pl.ds(main_lane(py, px), 256)]
        remote(src, x_two.at[own_rows], x2_s.at[k], x2_r.at[u], (e, 4 * py + px)).start()

    @pl.loop(1, 16)
    def _(k):
        py, px, pu = plane_peer(k)
        src = tokens.at[:, pl.ds(main_lane(py, px) + 256, 128)]
        remote(src, x_one.at[own_rows], x1_s.at[k], x1_r.at[u], (e, 4 * py + px)).start()

    @pl.loop(1, 16)
    def _(k):
        py, px, pu = plane_peer(k)
        remote(dg_own, dg_in.at[pu], dg_s.at[k], dg_r.at[pu], (e, 4 * py + px)).wait_recv()

    dg_mid[...] = jnp.sum(dg_in[...], axis=0)

    @pl.loop(1, 16)
    def _(k):
        pe = (e + k) % 16
        src = dg_mid.at[pl.ds(pl.multiple_of(8 * (pe // 8), 8), 8)]
        remote(src, dg_fin.at[e], dgz_s.at[k], dgz_r.at[e], (pe, t)).start()

    dg_fin[pl.ds(e, 1)] = dg_mid[pl.ds(pl.multiple_of(8 * (e // 8), 8), 8), :][None]

    get_w.wait()
    get_h.wait()
    wide = w_v[:, 0:PANEL].astype(F32).T
    work[...] = wide
    step = jnp.max(jnp.abs(wide), axis=0, keepdims=True) / 7.0 + 1e-06
    cols = lax.broadcasted_iota(jnp.int32, (PANEL, PANEL), 0)
    rows = lax.broadcasted_iota(jnp.int32, (PANEL, PANEL), 1)
    ht[...] = jnp.where(cols > rows, h_v[:, 0:PANEL].T, 0.0)
    dinv[...] = 1.0 / jnp.broadcast_to(hdiag[...], (PANEL, PANEL)).T

    @pl.loop(1, 16)
    def _(k):
        pe = (e + k) % 16
        src = dg_mid.at[pl.ds(pl.multiple_of(8 * (e // 8), 8), 8)]
        remote(src, dg_fin.at[pe], dgz_s.at[k], dgz_r.at[pe], (pe, t)).wait_recv()

    eight = jnp.sum(dg_fin[...], axis=0)
    this = lax.broadcasted_iota(jnp.int32, (8, 128), 0) == e % 8
    dgram = jnp.sum(jnp.where(this, eight, 0.0), axis=0, keepdims=True) * SCALE
    colfac = jnp.sqrt(jnp.mean(dgram, axis=1, keepdims=True) / (dgram + 1e-05))
    grid_step = jnp.broadcast_to(colfac, (PANEL, PANEL)).T * step
    amp[...] = grid_step / (2.0 * math.pi)
    inv[...] = 1.0 / grid_step

    def round_columns(b):
        j0 = pl.multiple_of(b * 8, 8)
        at = pl.ds(j0, 8)
        rot[...] = pltpu.roll(ht[...], (PANEL - b * 8) % PANEL, 1)
        near = rot[at, :]
        block = work[at, :]
        inv_b, amp_b, dinv_b = inv[at, :], amp[at, :], dinv[at, :]
        row = lax.broadcasted_iota(jnp.int32, (8, 128), 0)
        faults = []
        fault_rows = jnp.zeros((8, 128), F32)
        for j in range(8):
            value = jnp.broadcast_to(block[j : j + 1], (8, 128))
            turns = value * jnp.broadcast_to(inv_b[j : j + 1], (8, 128))
            moved = sine_of_turns(turns) * jnp.broadcast_to(amp_b[j : j + 1], (8, 128))
            fault = moved * jnp.broadcast_to(dinv_b[j : j + 1], (8, 128))
            coef = jnp.broadcast_to(near[:, j : j + 1], (8, 128))
            block = jnp.where(row == j, value - moved, block - fault * coef)
            fault_rows = jnp.where(row == j, fault, fault_rows)
            faults.append(fault)
        for k in range(16):
            part = pl.ds(8 * k, 8)
            acc = work[part, :]
            for j in range(8):
                acc = acc - faults[j] * jnp.broadcast_to(rot[part, j : j + 1], (8, 128))
            work[part, :] = acc
        work[at, :] = block
        errs[at, :] = fault_rows

    @pl.loop(0, 8)
    def _(b):
        round_columns(b)

    @pl.loop(1, 4)
    def _(k):
        px = (x + k) % 4
        theirs = pl.ds(4 * place_of(px), 4)
        remote(msg.at[theirs], msg.at[theirs], pb_s.at[k], pb_r.at[px], (e, 4 * y + px)).wait_recv()

    def mask_panels(half):
        for pu in range(8):
            sender = 8 * half + pu
            their = msg[sender, 0:PANEL, :]
            flags = msg[sender, PANEL:MSG, :]
            for s in range(SLOTS):
                side_row = jnp.where(c == s % 2, 1, 0)
                value = their * jnp.broadcast_to(flags[s : s + 1], (PANEL, TOK))
                mt[
                    half,
                    pl.ds(pl.multiple_of(side_row * 1024 + (s // 2) * PANEL, PANEL), PANEL),
                    pl.ds(pu * TOK, TOK),
                ] = value

    @pl.loop(0, 2)
    def _(half):
        mask_panels(half)

    def partial_rows(m, source, is_left):
        at = pl.ds(pl.multiple_of(m * 256, 256), 256)
        if is_left:
            return jnp.dot(mt[group, at, :], source[...], preferred_element_type=F32)
        return jnp.dot(mt[0, at, :], source[pl.ds(0, 1024), :], preferred_element_type=F32) + jnp.dot(
            mt[1, at, :], source[pl.ds(1024, 1024), :], preferred_element_type=F32
        )

    def grams(index, lane, width, source, is_left):
        lanes = pl.ds(lane, width)

        @pl.loop(0, 4)
        def _(m):
            at = pl.ds(pl.multiple_of(m * 256, 256), 256)
            sib_out[at, lanes] = partial_rows(m, source, is_left).astype(BF16)

        swap = remote(
            sib_out.at[:, lanes],
            sib_in.at[:, lanes],
            sib_s.at[index],
            sib_r.at[index],
            (2 * z + 1 - c, t),
        )
        swap.start()

        @pl.loop(0, 4)
        def _(m):
            at = pl.ds(pl.multiple_of(m * 256, 256), 256)
            own[at, lanes] = partial_rows(m + 4, source, is_left)

        swap.wait_recv()

        @pl.loop(0, 7)
        def _(i):
            pz = z_peer(i)
            at = pl.ds(pl.multiple_of(pz * PANEL, PANEL), PANEL)
            both = own[at, lanes] + sib_in[at, lanes].astype(F32)
            z_out[pl.ds(pz, 1), :, lanes] = both.astype(BF16)[None]
            remote(
                z_out.at[pz, :, lanes],
                z_in.at[z, :, lanes],
                z_s.at[index, i],
                z_r.at[index, z],
                (2 * pz + c, t),
            ).start()

        at = pl.ds(pl.multiple_of(z * PANEL, PANEL), PANEL)
        fin[:, lanes] = own[at, lanes] + sib_in[at, lanes].astype(F32)

    def gather_sum(index, lane, width):
        lanes = pl.ds(lane, width)

        @pl.loop(0, 7)
        def _(i):
            pz = z_peer(i)
            remote(
                z_out.at[pz, :, lanes],
                z_in.at[pz, :, lanes],
                z_s.at[index, i],
                z_r.at[index, pz],
                (2 * pz + c, t),
            ).wait_recv()
            fin[:, lanes] += z_in[pl.ds(pz, 1), :, lanes][0].astype(F32)

    @pl.loop(0, 8)
    def _(k):
        py, m = (y + k // 2) % 4, k % 2
        px = left_x(m)
        pu = 4 * place_of(px) + py - 8 * group
        theirs = pl.ds(pl.multiple_of(pu * TOK, TOK), TOK)
        src = tokens.at[:, pl.ds(left_lane(py, m), 128)]
        itself = (py == y) & (px == x)

        @pl.when(jnp.logical_not(itself))
        def _():
            remote(src, x_left.at[theirs], xl_s.at[k], xl_r.at[pu], (e, 4 * py + px)).wait_recv()

        @pl.when(itself)
        def _():
            pltpu.make_async_copy(src, x_left.at[theirs], local_sem.at[3]).wait()

    grams(0, 0, 128, x_left, True)

    @pl.loop(8, 16)
    def _(b):
        round_columns(b)

    keep_two.wait()

    @pl.loop(1, 16)
    def _(k):
        py, px, pu = plane_peer(k)
        src = tokens.at[:, pl.ds(main_lane(py, px), 256)]
        theirs = pl.ds(pl.multiple_of(pu * TOK, TOK), TOK)
        remote(src, x_two.at[theirs], x2_s.at[k], x2_r.at[pu], (e, 4 * py + px)).wait_recv()

    grams(1, 128, 256, x_two, False)

    err_rows = errs[...].T.astype(BF16)

    @pl.loop(0, 14)
    def _(i):
        lanes = pl.ds(pl.multiple_of(i * 512, 512), 512)
        fix = jnp.dot(err_rows, h_v[:, lanes].astype(BF16), preferred_element_type=F32)
        out_v[:, lanes] = (w_v[:, lanes].astype(F32) - fix).astype(BF16)

    out_v[:, 0:PANEL] = work[...].T.astype(BF16)
    put_out = pltpu.make_async_copy(out_v, updated, local_sem.at[6])
    put_out.start()

    gather_sum(0, 0, 128)
    left[...] = fin[:, 0:128].T * SCALE
    half_rows = pl.ds(pl.multiple_of((1 - side) * 64, 64), 64)
    left_out[...] = left[half_rows, :]
    swap_left = remote(left_out, left_in, lx_s.at[0], lx_r.at[0], (e, 4 * y + x + 1 - 2 * side))
    swap_left.start()

    keep_one.wait()

    @pl.loop(1, 16)
    def _(k):
        py, px, pu = plane_peer(k)
        src = tokens.at[:, pl.ds(main_lane(py, px) + 256, 128)]
        theirs = pl.ds(pl.multiple_of(pu * TOK, TOK), TOK)
        remote(src, x_one.at[theirs], x1_s.at[k], x1_r.at[pu], (e, 4 * py + px)).wait_recv()

    grams(2, 384, 128, x_one, False)

    base = 64 * side
    gather_sum(1, 128, 256)
    gram[pl.ds(pl.multiple_of(base, 64), 256), :] = fin[:, 128:384].T * SCALE
    swap_left.wait_recv()
    left_at = pl.ds(pl.multiple_of(384 * (1 - side), 64), 64)
    gram[left_at, :] = left[pl.ds(pl.multiple_of(side * 64, 64), 64), :] + left_in[...]
    gather_sum(2, 384, 128)
    gram[pl.ds(pl.multiple_of(base + 256, 64), 128), :] = fin[:, 384:512].T * SCALE

    @pl.loop(1, 16)
    def _(k):
        py, px, pu = plane_peer(k)
        to = (e, 4 * py + px)
        pe = (e + k) % 16
        remote(dg_own, dg_in.at[u], dg_s.at[k], dg_r.at[u], to).wait_send()
        src = dg_mid.at[pl.ds(pl.multiple_of(8 * (pe // 8), 8), 8)]
        remote(src, dg_fin.at[e], dgz_s.at[k], dgz_r.at[e], (pe, t)).wait_send()
        src = tokens.at[:, pl.ds(main_lane(py, px), 256)]
        remote(src, x_two.at[own_rows], x2_s.at[k], x2_r.at[u], to).wait_send()
        src = tokens.at[:, pl.ds(main_lane(py, px) + 256, 128)]
        remote(src, x_one.at[own_rows], x1_s.at[k], x1_r.at[u], to).wait_send()

    @pl.loop(1, 4)
    def _(k):
        to = (e, 4 * ((y + k) % 4) + x)
        remote(msg.at[u], msg.at[u], pa_s.at[k], pa_r.at[y], to).wait_send()
        to = (e, 4 * y + (x + k) % 4)
        remote(msg.at[mine], msg.at[mine], pb_s.at[k], pb_r.at[x], to).wait_send()

    @pl.loop(0, 8)
    def _(k):
        py, m = (y + k // 2) % 4, k % 2
        px = left_x(m)
        src = tokens.at[:, pl.ds(left_lane(py, m), 128)]

        @pl.when(jnp.logical_not((py == y) & (px == x)))
        def _():
            to = (e, 4 * py + px)
            remote(src, x_left.at[left_rows], xl_s.at[k], xl_r.at[u - 8 * group], to).wait_send()

    for index, lane, width in ((0, 0, 128), (1, 128, 256), (2, 384, 128)):
        lanes = pl.ds(lane, width)
        remote(
            sib_out.at[:, lanes],
            sib_in.at[:, lanes],
            sib_s.at[index],
            sib_r.at[index],
            (2 * z + 1 - c, t),
        ).wait_send()

        @pl.loop(0, 7)
        def _(i):
            pz = z_peer(i)
            remote(
                z_out.at[pz, :, lanes],
                z_in.at[z, :, lanes],
                z_s.at[index, i],
                z_r.at[index, z],
                (2 * pz + c, t),
            ).wait_send()

    swap_left.wait_send()
    put_out.wait()


def body(tokens, routes, owner_of, weights, hinv_diag, hinv_rows):
    vmem = pl.BlockSpec(memory_space=pltpu.VMEM)
    hbm = pl.BlockSpec(memory_space=pl.ANY)
    dma = pltpu.SemaphoreType.DMA
    square = pltpu.VMEM((PANEL, PANEL), F32)
    gram, updated = pl.pallas_call(
        kernel,
        out_shape=(
            jax.ShapeDtypeStruct((SHARE, PANEL), F32),
            jax.ShapeDtypeStruct((128, D), BF16),
        ),
        in_specs=[hbm, vmem, pl.BlockSpec(memory_space=pltpu.SMEM), hbm, vmem, hbm],
        out_specs=(vmem, hbm),
        scratch_shapes=[
            pltpu.VMEM((TOK, 128), BF16),
            pltpu.VMEM((PLANE, MSG, TOK), BF16),
            pltpu.VMEM((128, D), BF16),
            pltpu.VMEM((PANEL, D), F32),
            pltpu.VMEM((128, D), BF16),
            pltpu.VMEM((SLOTS, PANEL), F32),
            pltpu.VMEM((PLANE, SLOTS, PANEL), F32),
            pltpu.VMEM((SLOTS, PANEL), F32),
            pltpu.VMEM((16, 8, PANEL), F32),
            pltpu.VMEM((2, SLOTS * PANEL, 8 * TOK), BF16),
            pltpu.VMEM((8 * TOK, 128), BF16),
            pltpu.VMEM((PLANE * TOK, 256), BF16),
            pltpu.VMEM((PLANE * TOK, 128), BF16),
            square,
            square,
            square,
            square,
            square,
            square,
            square,
            pltpu.VMEM((RING * PANEL, 512), BF16),
            pltpu.VMEM((RING * PANEL, 512), BF16),
            pltpu.VMEM((RING * PANEL, 512), F32),
            pltpu.VMEM((RING, PANEL, 512), BF16),
            pltpu.VMEM((RING, PANEL, 512), BF16),
            pltpu.VMEM((PANEL, 512), F32),
            square,
            pltpu.VMEM((64, PANEL), F32),
            pltpu.VMEM((64, PANEL), F32),
            dma((8,)),
            dma((16,)),
            dma((16,)),
            dma((16,)),
            dma((16,)),
            dma((4,)),
            dma((4,)),
            dma((4,)),
            dma((4,)),
            dma((8,)),
            dma((8,)),
            dma((16,)),
            dma((16,)),
            dma((16,)),
            dma((16,)),
            dma((3,)),
            dma((3,)),
            dma((3, 7)),
            dma((3, 8)),
            dma((1,)),
            dma((1,)),
        ],
        compiler_params=pltpu.CompilerParams(
            collective_id=0, has_side_effects=True, vmem_limit_bytes=56 * 2**20
        ),
        cost_estimate=pl.CostEstimate(flops=4 * 10**9, bytes_accessed=10**7, transcendentals=0),
        name="calibrate",
    )(tokens, routes, owner_of, weights[0], hinv_diag, hinv_rows[0])
    return gram[None], updated[None]


def solution(mesh):
    in_specs = (
        P(("expert", "token"), None),
        P(("expert", "token"), None),
        P(),
        P("expert", "token", None),
        P("expert", None),
        P("expert", None, None),
    )
    out_specs = (P("expert", "token", None), P("expert", "token", None))
    return jax.shard_map(body, mesh=mesh, in_specs=in_specs, out_specs=out_specs, check_vma=False)
```

```python
import math

import jax
import jax.numpy as jnp
from jax import lax
from jax.experimental import pallas as pl
from jax.experimental.pallas import tpu as pltpu
from jax.sharding import PartitionSpec as P

D = 7168
PANEL = 128
TOP = 2
TOK = 128
SLOTS = 16
RING = 8
PLANE = 16
SHARE = 448
MSG = PANEL + SLOTS
MESH = pl.DeviceIdType.MESH
BF16 = jnp.bfloat16
F32 = jnp.float32
SCALE = 16.0 / 65536.0

SINE = (
    6.2831852700170625,
    -16.20895564378196,
    16.769189671870134,
    -9.624604702175908,
    3.5163760294927235,
    -0.7983429889808796,
)


def sine_of_turns(turns):
    r = turns - jnp.round(turns)
    y = r * r
    y2 = y * y
    low = SINE[0] + SINE[1] * y
    mid = SINE[2] + SINE[3] * y
    top = SINE[4] + SINE[5] * y
    edge = r - 4.0 * (r * y)
    return edge * (low + y2 * (mid + y2 * top))


def place_of(x):
    return jnp.where(x == 0, 0, jnp.where(x == 3, 1, x + 1))


def kernel(
    tokens,
    routes,
    owner,
    weights,
    hdiag,
    hrows,
    gram,
    updated,
    x0,
    msg,
    w_v,
    h_v,
    dg_own,
    dg_in,
    dg_mid,
    dg_fin,
    mt,
    x_left,
    x_two,
    x_one,
    ht,
    rot,
    work,
    inv,
    amp,
    dinv,
    errs,
    sib_out,
    sib_in,
    own,
    z_out,
    z_in,
    hold,
    fin,
    left,
    left_out,
    left_in,
    local_sem,
    dg_s,
    dg_r,
    dgz_s,
    dgz_r,
    pm_s,
    pm_r,
    xl_s,
    xl_r,
    xm_s,
    xm_r,
    sib_s,
    sib_r,
    z_s,
    z_r,
    lx_s,
    lx_r,
):
    e = lax.axis_index("expert")
    t = lax.axis_index("token")
    z, c = e // 2, e % 2
    y, x = t // 4, t % 4
    place = place_of(x)
    u = 4 * place + y
    group = place // 2
    side = x % 2

    ys = [y] + [(y + k) % 4 for k in range(1, 4)]
    xs = [x, 3 - x, (x + 2) % 4, (5 - x) % 4]
    places = [place] + [place_of(px) for px in xs[1:]]
    plane = [(ys[k // 4], xs[k % 4], 4 * places[k % 4] + ys[k // 4]) for k in range(16)]
    others = plane[1:]
    near_first = [k for k in range(1, 16) if k % 4 < 2] + [k for k in range(1, 16) if k % 4 >= 2]
    half_ring = [plane[4 * (k // 2) + k % 2] for k in range(8)]
    experts = [(e + k) % 16 for k in range(1, 16)]

    def ring(steps):
        return (z + jnp.where(c == 0, steps % RING, -steps % RING)) % RING

    def tile_rows(index):
        return pl.ds(pl.multiple_of(index * TOK, TOK), TOK)

    def main_lanes(py, px, part):
        first = 7 * (2 * py + px // 2) + 4 * (px % 2) + 2 * part
        return pl.ds(pl.multiple_of(first * 128, 128), 256 - 128 * part)

    def stage_lanes(index):
        return (pl.ds(0, 128), pl.ds(128, 256), pl.ds(384, 128))[index]

    def left_lanes(py, px):
        return pl.ds(pl.multiple_of((7 * (2 * py + px // 2) + 3) * 128, 128), 128)

    def remote(src, dst, send, recv, device):
        return pltpu.make_async_remote_copy(
            src_ref=src,
            dst_ref=dst,
            send_sem=send,
            recv_sem=recv,
            device_id=device,
            device_id_type=MESH,
        )

    sent = []

    def start(copy):
        copy.start()
        sent.append(copy)

    barrier = pltpu.get_barrier_semaphore()
    for py, px, _ in others:
        pl.semaphore_signal(barrier, inc=1, device_id=(e, 4 * py + px), device_id_type=MESH)
    for pe in experts:
        pl.semaphore_signal(barrier, inc=1, device_id=(pe, t), device_id_type=MESH)

    get_x0 = pltpu.make_async_copy(tokens.at[:, pl.ds(0, 128)], x0, local_sem.at[0])
    get_w = pltpu.make_async_copy(weights, w_v, local_sem.at[1])
    get_h = pltpu.make_async_copy(hrows, h_v, local_sem.at[2])
    get_x0.start()
    get_w.start()
    get_h.start()

    first = jnp.broadcast_to(routes[0:1, :], (SLOTS, TOK))
    second = jnp.broadcast_to(routes[1:2, :], (SLOTS, TOK))
    slot_a = jnp.zeros((SLOTS, TOK), jnp.int32)
    slot_b = jnp.zeros((SLOTS, TOK), jnp.int32)
    for i in range(SLOTS):
        slot_a = jnp.where(first == i, owner[i], slot_a)
        slot_b = jnp.where(second == i, owner[i], slot_b)
    slot_row = lax.broadcasted_iota(jnp.int32, (SLOTS, TOK), 0)
    mask = jnp.where((slot_a == slot_row) | (slot_b == slot_row), 1.0, 0.0).astype(F32)

    get_x0.wait()
    panel = x0[...].astype(F32)
    square = panel * panel
    high = square.astype(BF16)
    low = (square - high.astype(F32)).astype(BF16)
    mask16 = mask.astype(BF16)
    dg_own[...] = jnp.dot(mask16, high, preferred_element_type=F32) + jnp.dot(
        mask16, low, preferred_element_type=F32
    )
    msg[pl.ds(u, 1), pl.ds(0, PANEL), :] = panel.T.astype(BF16)[None]
    msg[pl.ds(u, 1), pl.ds(PANEL, SLOTS), :] = mask16[None]

    pl.semaphore_wait(barrier, 30)

    for k, (py, px, _) in enumerate(others):
        start(remote(dg_own, dg_in.at[u], dg_s.at[k], dg_r.at[u], (e, 4 * py + px)))
    for k in near_first:
        py, px, _ = plane[k]
        start(remote(msg.at[u], msg.at[u], pm_s.at[k], pm_r.at[u], (e, 4 * py + px)))
    for k, (py, px, _) in enumerate(half_ring):
        src = tokens.at[:, left_lanes(py, px)]
        dst = x_left.at[tile_rows(u - 8 * group)]
        if k == 0:
            keep_left = pltpu.make_async_copy(src, dst, local_sem.at[3])
            keep_left.start()
        else:
            start(remote(src, dst, xl_s.at[k], xl_r.at[u - 8 * group], (e, 4 * py + px)))

    x_main = (x_two, x_one)
    keeps = []
    for part in range(2):
        keep = pltpu.make_async_copy(
            tokens.at[:, main_lanes(y, x, part)], x_main[part].at[tile_rows(u)], local_sem.at[4 + part]
        )
        keep.start()
        keeps.append(keep)
    dg_in[pl.ds(u, 1)] = dg_own[...][None]

    for part in range(2):
        for k, (py, px, _) in enumerate(others):
            src = tokens.at[:, main_lanes(py, px, part)]
            dst = x_main[part].at[tile_rows(u)]
            start(remote(src, dst, xm_s.at[part, k], xm_r.at[part, u], (e, 4 * py + px)))

    get_w.wait()
    get_h.wait()
    wide = w_v[:, 0:PANEL].astype(F32).T
    work[...] = wide
    step = jnp.max(jnp.abs(wide), axis=0, keepdims=True) / 7.0 + 1e-06
    cols = lax.broadcasted_iota(jnp.int32, (PANEL, PANEL), 0)
    rows = lax.broadcasted_iota(jnp.int32, (PANEL, PANEL), 1)
    ht[...] = jnp.where(cols > rows, h_v[:, 0:PANEL].T, 0.0)
    dinv[...] = 1.0 / jnp.broadcast_to(hdiag[...], (PANEL, PANEL)).T

    def mask_panel(sender):
        their = msg[sender, 0:PANEL, :]
        flags = msg[sender, PANEL:MSG, :]
        lanes = tile_rows(sender)
        for s in range(SLOTS):
            value = their * jnp.broadcast_to(flags[s : s + 1], (PANEL, TOK))
            at = jnp.where(c == s % 2, 1024, 0) + (s // 2) * PANEL
            mt[pl.ds(pl.multiple_of(at, PANEL), PANEL), lanes] = value

    def arrived_panels(column):
        @pl.loop(0, 4)
        def _(i):
            sender = 4 * places[column] + (y + i) % 4

            @pl.when(sender != u)
            def _():
                to = (e, 4 * ((y + i) % 4) + xs[column])
                remote(msg.at[sender], msg.at[sender], pm_s.at[0], pm_r.at[sender], to).wait_recv()

            mask_panel(sender)

    for k, (py, px, pu) in enumerate(others):
        remote(dg_own, dg_in.at[pu], dg_s.at[k], dg_r.at[pu], (e, 4 * py + px)).wait_recv()
    dg_mid[...] = jnp.sum(dg_in[...], axis=0)
    for k, pe in enumerate(experts):
        src = dg_mid.at[pl.ds(pl.multiple_of(8 * (pe // 8), 8), 8)]
        start(remote(src, dg_fin.at[e], dgz_s.at[k], dgz_r.at[e], (pe, t)))
    my_eight = pl.ds(pl.multiple_of(8 * (e // 8), 8), 8)
    dg_fin[pl.ds(e, 1)] = dg_mid[my_eight, :][None]

    arrived_panels(0)
    arrived_panels(1)

    def grams(index, source, is_left, meanwhile=lambda: None):
        lanes = stage_lanes(index)

        def product(first_row):
            if is_left:
                left_mt = mt[pl.ds(first_row, 1024), pl.ds(pl.multiple_of(group * 1024, 1024), 1024)]
                return jnp.dot(left_mt, source[...], preferred_element_type=F32)
            return jnp.dot(mt[pl.ds(first_row, 1024), :], source[...], preferred_element_type=F32)

        sib_out[:, lanes] = product(0).astype(BF16)
        swap = remote(
            sib_out.at[:, lanes],
            sib_in.at[:, lanes],
            sib_s.at[index],
            sib_r.at[index],
            (2 * z + 1 - c, t),
        )
        start(swap)
        own[:, lanes] = product(1024)
        meanwhile()
        swap.wait_recv()

        def block(steps):
            at = tile_rows(ring(steps))
            return own[at, lanes] + sib_in[at, lanes].astype(F32)

        for kind, (target, to) in enumerate(((-4, -2), (-3, -1), (3, 1), (-1, -1), (1, 1))):
            z_out[kind, :, lanes] = block(target).astype(BF16)
            start(z_copy(index, kind, to))
        hold[0, :, lanes] = block(-2)
        hold[1, :, lanes] = block(2)
        fin[:, lanes] = block(0)

    def z_copy(index, kind, steps):
        lanes = stage_lanes(index)
        return remote(
            z_out.at[kind, :, lanes],
            z_in.at[kind, :, lanes],
            z_s.at[index, kind],
            z_r.at[index, kind],
            (2 * ring(steps) + c, t),
        )

    def relay(index):
        lanes = stage_lanes(index)
        z_copy(index, 0, 2).wait_recv()
        z_copy(index, 1, 1).wait_recv()
        far = z_in[0, :, lanes].astype(F32) + z_in[1, :, lanes].astype(F32)
        z_out[5, :, lanes] = (hold[0, :, lanes] + far).astype(BF16)
        start(z_copy(index, 5, -2))
        z_copy(index, 2, -1).wait_recv()
        z_out[6, :, lanes] = (hold[1, :, lanes] + z_in[2, :, lanes].astype(F32)).astype(BF16)
        start(z_copy(index, 6, 2))

    def gather_sum(index):
        lanes = stage_lanes(index)
        acc = fin[:, lanes]
        for kind, steps in ((3, 1), (4, -1), (5, 2), (6, -2)):
            z_copy(index, kind, steps).wait_recv()
            acc = acc + z_in[kind, :, lanes].astype(F32)
        return acc.T * SCALE

    for k, pe in enumerate(experts):
        src = dg_mid.at[my_eight]
        remote(src, dg_fin.at[pe], dgz_s.at[k], dgz_r.at[pe], (pe, t)).wait_recv()
    eight = jnp.sum(dg_fin[...], axis=0)
    this = lax.broadcasted_iota(jnp.int32, (8, 128), 0) == e % 8
    dgram = jnp.sum(jnp.where(this, eight, 0.0), axis=0, keepdims=True) * SCALE
    colfac = jnp.sqrt(jnp.mean(dgram, axis=1, keepdims=True) / (dgram + 1e-05))
    grid_step = jnp.broadcast_to(colfac, (PANEL, PANEL)).T * step
    amp[...] = grid_step / (2.0 * math.pi)
    inv[...] = 1.0 / grid_step

    def round_columns(b):
        j0 = pl.multiple_of(b * 8, 8)
        at = pl.ds(j0, 8)
        rot[...] = pltpu.roll(ht[...], (PANEL - b * 8) % PANEL, 1)
        near = rot[at, :]
        block = work[at, :]
        inv_b, amp_b, dinv_b = inv[at, :], amp[at, :], dinv[at, :]
        row = lax.broadcasted_iota(jnp.int32, (8, 128), 0)
        faults = []
        fault_rows = jnp.zeros((8, 128), F32)
        for j in range(8):
            value = jnp.broadcast_to(block[j : j + 1], (8, 128))
            turns = value * jnp.broadcast_to(inv_b[j : j + 1], (8, 128))
            moved = sine_of_turns(turns) * jnp.broadcast_to(amp_b[j : j + 1], (8, 128))
            fault = moved * jnp.broadcast_to(dinv_b[j : j + 1], (8, 128))
            coef = jnp.broadcast_to(near[:, j : j + 1], (8, 128))
            block = jnp.where(row == j, value - moved, block - fault * coef)
            fault_rows = jnp.where(row == j, fault, fault_rows)
            faults.append(fault)
        for k in range(16):
            part = pl.ds(8 * k, 8)
            acc = work[part, :]
            for j in range(8):
                acc = acc - faults[j] * jnp.broadcast_to(rot[part, j : j + 1], (8, 128))
            work[part, :] = acc
        work[at, :] = block
        errs[at, :] = fault_rows

    @pl.loop(0, 16)
    def _(b):
        round_columns(b)

    def arrived_part(part):
        keeps[part].wait()
        for k, (py, px, pu) in enumerate(others):
            src = tokens.at[:, main_lanes(py, px, part)]
            dst = x_main[part].at[tile_rows(pu)]
            remote(src, dst, xm_s.at[part, k], xm_r.at[part, pu], (e, 4 * py + px)).wait_recv()

    arrived_panels(2)
    arrived_panels(3)

    for k, (py, px, pu) in enumerate(half_ring):
        if k == 0:
            keep_left.wait()
        else:
            src = tokens.at[:, left_lanes(py, px)]
            dst = x_left.at[tile_rows(pu - 8 * group)]
            remote(src, dst, xl_s.at[k], xl_r.at[pu - 8 * group], (e, 4 * py + px)).wait_recv()
    grams(0, x_left, True)


    err_rows = errs[...].T.astype(BF16)

    @pl.loop(0, 14)
    def _(i):
        lanes = pl.ds(pl.multiple_of(i * 512, 512), 512)
        fix = jnp.dot(err_rows, h_v[:, lanes].astype(BF16), preferred_element_type=F32)
        updated[:, lanes] = (w_v[:, lanes].astype(F32) - fix).astype(BF16)

    updated[:, 0:PANEL] = work[...].T.astype(BF16)
    relay(0)

    arrived_part(0)
    grams(1, x_two, False)

    left[...] = gather_sum(0)
    half_rows = pl.ds(pl.multiple_of((1 - side) * 64, 64), 64)
    left_out[...] = left[half_rows, :]
    swap_left = remote(left_out, left_in, lx_s.at[0], lx_r.at[0], (e, 4 * y + x + 1 - 2 * side))
    start(swap_left)

    arrived_part(1)
    grams(2, x_one, False, lambda: relay(1))

    base = 64 * side
    swap_left.wait_recv()
    left_at = pl.ds(pl.multiple_of(384 * (1 - side), 64), 64)
    gram[left_at, :] = left[pl.ds(pl.multiple_of(side * 64, 64), 64), :] + left_in[...]
    gram[pl.ds(pl.multiple_of(base, 64), 256), :] = gather_sum(1)
    relay(2)
    gram[pl.ds(pl.multiple_of(base + 256, 64), 128), :] = gather_sum(2)

    for copy in sent:
        copy.wait_send()


def body(tokens, routes, owner_of, weights, hinv_diag, hinv_rows):
    vmem = pl.BlockSpec(memory_space=pltpu.VMEM)
    hbm = pl.BlockSpec(memory_space=pl.ANY)
    dma = pltpu.SemaphoreType.DMA
    square = pltpu.VMEM((PANEL, PANEL), F32)
    gram, updated = pl.pallas_call(
        kernel,
        out_shape=(pltpu.VMEM((SHARE, PANEL), F32), pltpu.VMEM((128, D), BF16)),
        in_specs=[hbm, vmem, pl.BlockSpec(memory_space=pltpu.SMEM), hbm, vmem, hbm],
        out_specs=(vmem, vmem),
        scratch_shapes=[
            pltpu.VMEM((TOK, 128), BF16),
            pltpu.VMEM((PLANE, MSG, TOK), BF16),
            pltpu.VMEM((128, D), BF16),
            pltpu.VMEM((PANEL, D), F32),
            pltpu.VMEM((SLOTS, PANEL), F32),
            pltpu.VMEM((PLANE, SLOTS, PANEL), F32),
            pltpu.VMEM((SLOTS, PANEL), F32),
            pltpu.VMEM((16, 8, PANEL), F32),
            pltpu.VMEM((SLOTS * PANEL, PLANE * TOK), BF16),
            pltpu.VMEM((8 * TOK, 128), BF16),
            pltpu.VMEM((PLANE * TOK, 256), BF16),
            pltpu.VMEM((PLANE * TOK, 128), BF16),
            square,
            square,
            square,
            square,
            square,
            square,
            square,
            pltpu.VMEM((RING * PANEL, 512), BF16),
            pltpu.VMEM((RING * PANEL, 512), BF16),
            pltpu.VMEM((RING * PANEL, 512), F32),
            pltpu.VMEM((7, PANEL, 512), BF16),
            pltpu.VMEM((7, PANEL, 512), BF16),
            pltpu.VMEM((2, PANEL, 512), F32),
            pltpu.VMEM((PANEL, 512), F32),
            square,
            pltpu.VMEM((64, PANEL), F32),
            pltpu.VMEM((64, PANEL), F32),
            dma((8,)),
            dma((15,)),
            dma((16,)),
            dma((15,)),
            dma((16,)),
            dma((16,)),
            dma((16,)),
            dma((8,)),
            dma((8,)),
            dma((2, 15)),
            dma((2, 16)),
            dma((3,)),
            dma((3,)),
            dma((3, 7)),
            dma((3, 7)),
            dma((1,)),
            dma((1,)),
        ],
        compiler_params=pltpu.CompilerParams(
            collective_id=0, has_side_effects=True, vmem_limit_bytes=61 * 2**20
        ),
        cost_estimate=pl.CostEstimate(flops=4 * 10**9, bytes_accessed=10**7, transcendentals=0),
        name="calibrate",
    )(tokens, routes.T, owner_of, weights[0], hinv_diag, hinv_rows[0])
    return gram[None], updated[None]


def solution(mesh):
    in_specs = (
        P(("expert", "token"), None),
        P(("expert", "token"), None),
        P(),
        P("expert", "token", None),
        P("expert", None),
        P("expert", None, None),
    )
    out_specs = (P("expert", "token", None), P("expert", "token", None))
    return jax.shard_map(body, mesh=mesh, in_specs=in_specs, out_specs=out_specs, check_vma=False)
```

```python
import math

import jax
import jax.numpy as jnp
from jax import lax
from jax.experimental import pallas as pl
from jax.experimental.pallas import tpu as pltpu
from jax.sharding import PartitionSpec as P

D = 7168
PANEL = 128
TOP = 2
TOK = 128
SLOTS = 16
RING = 8
PLANE = 16
SHARE = 448
MSG = PANEL + SLOTS
MESH = pl.DeviceIdType.MESH
BF16 = jnp.bfloat16
F32 = jnp.float32
SCALE = 16.0 / 65536.0

SINE = (
    6.2831852700170625,
    -16.20895564378196,
    16.769189671870134,
    -9.624604702175908,
    3.5163760294927235,
    -0.7983429889808796,
)


def sine_of_turns(turns):
    r = turns - jnp.round(turns)
    y = r * r
    y2 = y * y
    low = SINE[0] + SINE[1] * y
    mid = SINE[2] + SINE[3] * y
    top = SINE[4] + SINE[5] * y
    edge = r - 4.0 * (r * y)
    return edge * (low + y2 * (mid + y2 * top))


DIRECT = (4, 3, -3, 2, -2, 1, -1)


def place_of(x):
    return jnp.where(x == 0, 0, jnp.where(x == 3, 1, x + 1))


def kernel(
    tokens,
    routes_in,
    owner_in,
    weights,
    hdiag_in,
    hrows,
    gram,
    updated,
    routes,
    owner,
    hdiag,
    x0,
    msg,
    w_v,
    h_v,
    h_half,
    dg_own,
    dg_in,
    dg_mid,
    dg_fin,
    mt,
    x_left,
    x_two,
    x_one,
    ht,
    rot,
    work,
    inv,
    amp,
    dinv,
    errs,
    sib_out,
    sib_in,
    own,
    z_out,
    z_in,
    hold,
    fin,
    left,
    left_out,
    left_in,
    local_sem,
    dg_s,
    dg_r,
    dgz_s,
    dgz_r,
    pm_s,
    pm_r,
    pc_s,
    pc_r,
    xl_s,
    xl_r,
    xm_s,
    xm_r,
    sib_s,
    sib_r,
    z_s,
    z_r,
    lx_s,
    lx_r,
):
    e = lax.axis_index("expert")
    t = lax.axis_index("token")
    z, c = e // 2, e % 2
    y, x = t // 4, t % 4
    place = place_of(x)
    u = 4 * place + y
    group = place // 2
    side = x % 2

    ys = [y] + [(y + k) % 4 for k in range(1, 4)]
    xs = [x, 3 - x, (x + 2) % 4, (5 - x) % 4]
    places = [place] + [place_of(px) for px in xs[1:]]
    plane = [(ys[k // 4], xs[k % 4], 4 * places[k % 4] + ys[k // 4]) for k in range(16)]
    others = plane[1:]
    half_ring = [plane[4 * (k // 2) + k % 2] for k in range(8)]
    experts = [(e + k) % 16 for k in range(1, 16)]

    def ring(steps):
        return (z + jnp.where(c == 0, steps % RING, -steps % RING)) % RING

    def tile_rows(index):
        return pl.ds(pl.multiple_of(index * TOK, TOK), TOK)

    def main_lanes(py, px, part):
        first = 7 * (2 * py + px // 2) + 4 * (px % 2) + 2 * part
        return pl.ds(pl.multiple_of(first * 128, 128), 256 - 128 * part)

    def stage_lanes(index):
        return (pl.ds(0, 128), pl.ds(128, 256), pl.ds(384, 128))[index]

    def left_lanes(py, px):
        return pl.ds(pl.multiple_of((7 * (2 * py + px // 2) + 3) * 128, 128), 128)

    def remote(src, dst, send, recv, device):
        return pltpu.make_async_remote_copy(
            src_ref=src,
            dst_ref=dst,
            send_sem=send,
            recv_sem=recv,
            device_id=device,
            device_id_type=MESH,
        )

    sent = []

    def start(copy):
        copy.start()
        sent.append(copy)

    barrier = pltpu.get_barrier_semaphore()
    for py, px, _ in others:
        pl.semaphore_signal(barrier, inc=1, device_id=(e, 4 * py + px), device_id_type=MESH)
    for pe in experts:
        pl.semaphore_signal(barrier, inc=1, device_id=(pe, t), device_id_type=MESH)

    get_x0 = pltpu.make_async_copy(tokens.at[:, pl.ds(0, 128)], x0, local_sem.at[0])
    get_w = pltpu.make_async_copy(weights, w_v, local_sem.at[1])
    get_h = pltpu.make_async_copy(hrows, h_v, local_sem.at[2])
    get_small = [
        pltpu.make_async_copy(routes_in, routes, local_sem.at[8]),
        pltpu.make_async_copy(owner_in, owner, local_sem.at[9]),
        pltpu.make_async_copy(hdiag_in, hdiag, local_sem.at[10]),
    ]
    for copy in get_small:
        copy.start()
    get_x0.start()
    get_w.start()
    get_h.start()

    for copy in get_small:
        copy.wait()
    first = jnp.broadcast_to(routes[0:1, :], (SLOTS, TOK))
    second = jnp.broadcast_to(routes[1:2, :], (SLOTS, TOK))
    slot_a = jnp.zeros((SLOTS, TOK), jnp.int32)
    slot_b = jnp.zeros((SLOTS, TOK), jnp.int32)
    for i in range(SLOTS):
        slot_a = jnp.where(first == i, owner[i], slot_a)
        slot_b = jnp.where(second == i, owner[i], slot_b)
    slot_row = lax.broadcasted_iota(jnp.int32, (SLOTS, TOK), 0)
    mask = jnp.where((slot_a == slot_row) | (slot_b == slot_row), 1.0, 0.0).astype(F32)

    get_x0.wait()
    panel = x0[...].astype(F32)
    square = panel * panel
    high = square.astype(BF16)
    low = (square - high.astype(F32)).astype(BF16)
    mask16 = mask.astype(BF16)
    dg_own[...] = jnp.dot(mask16, high, preferred_element_type=F32) + jnp.dot(
        mask16, low, preferred_element_type=F32
    )
    msg[pl.ds(u, 1), pl.ds(0, PANEL), :] = panel.T.astype(BF16)[None]
    msg[pl.ds(u, 1), pl.ds(PANEL, SLOTS), :] = mask16[None]

    pl.semaphore_wait(barrier, 30)

    for k, (py, px, _) in enumerate(others):
        start(remote(dg_own, dg_in.at[u], dg_s.at[k], dg_r.at[u], (e, 4 * py + px)))
    for k in range(1, 8):
        py, px, _ = half_ring[k]
        start(remote(msg.at[u], msg.at[u], pm_s.at[k], pm_r.at[u], (e, 4 * py + px)))
    for k, (py, px, _) in enumerate(half_ring):
        src = tokens.at[:, left_lanes(py, px)]
        dst = x_left.at[tile_rows(u - 8 * group)]
        if k == 0:
            keep_left = pltpu.make_async_copy(src, dst, local_sem.at[3])
            keep_left.start()
        else:
            start(remote(src, dst, xl_s.at[k], xl_r.at[u - 8 * group], (e, 4 * py + px)))

    x_main = (x_two, x_one)
    keeps = []
    for part in range(2):
        keep = pltpu.make_async_copy(
            tokens.at[:, main_lanes(y, x, part)], x_main[part].at[tile_rows(u)], local_sem.at[4 + part]
        )
        keep.start()
        keeps.append(keep)
    dg_in[pl.ds(u, 1)] = dg_own[...][None]

    for k in range(1, 4):
        pu = 4 * place + ys[k]
        remote(msg.at[pu], msg.at[pu], pm_s.at[0], pm_r.at[pu], (e, 4 * ys[k] + x)).wait_recv()
    column = pl.ds(4 * place, 4)
    for k in (2, 3):
        start(remote(msg.at[column], msg.at[column], pc_s.at[k], pc_r.at[x], (e, 4 * y + xs[k])))
    def send_part(part):
        for k, (py, px, _) in enumerate(others):
            src = tokens.at[:, main_lanes(py, px, part)]
            dst = x_main[part].at[tile_rows(u)]
            start(remote(src, dst, xm_s.at[part, k], xm_r.at[part, u], (e, 4 * py + px)))

    send_part(0)

    get_w.wait()
    get_h.wait()
    wide = w_v[:, 0:PANEL].astype(F32).T
    work[...] = wide
    step = jnp.max(jnp.abs(wide), axis=0, keepdims=True) / 7.0 + 1e-06
    cols = lax.broadcasted_iota(jnp.int32, (PANEL, PANEL), 0)
    rows = lax.broadcasted_iota(jnp.int32, (PANEL, PANEL), 1)
    ht[...] = jnp.where(cols > rows, h_v[:, 0:PANEL].T, 0.0)
    dinv[...] = 1.0 / jnp.broadcast_to(hdiag[...], (PANEL, PANEL)).T

    @pl.loop(0, 14)
    def _(i):
        lanes = pl.ds(pl.multiple_of(i * 512, 512), 512)
        h_half[:, lanes] = h_v[:, lanes].astype(BF16)


    def mask_panel(sender):
        their = msg[sender, 0:PANEL, :]
        flags = msg[sender, PANEL:MSG, :]
        lanes = tile_rows(sender)
        for s in range(SLOTS):
            value = their * jnp.broadcast_to(flags[s : s + 1], (PANEL, TOK))
            at = jnp.where(c == s % 2, 1024, 0) + (s // 2) * PANEL
            mt[pl.ds(pl.multiple_of(at, PANEL), PANEL), lanes] = value

    def arrived_panels(column):
        if column == 1:
            for k in range(4):
                pu = 4 * places[1] + ys[k]
                remote(msg.at[pu], msg.at[pu], pm_s.at[0], pm_r.at[pu], (e, 4 * ys[k] + xs[1])).wait_recv()
        if column > 1:
            theirs = pl.ds(4 * places[column], 4)
            px = xs[column]
            remote(msg.at[theirs], msg.at[theirs], pc_s.at[column], pc_r.at[px], (e, 4 * y + px)).wait_recv()

        @pl.loop(0, 4)
        def _(i):
            mask_panel(4 * places[column] + i)

    for k, (py, px, pu) in enumerate(others):
        remote(dg_own, dg_in.at[pu], dg_s.at[k], dg_r.at[pu], (e, 4 * py + px)).wait_recv()
    dg_mid[...] = jnp.sum(dg_in[...], axis=0)
    for k, pe in enumerate(experts):
        src = dg_mid.at[pl.ds(pl.multiple_of(8 * (pe // 8), 8), 8)]
        start(remote(src, dg_fin.at[e], dgz_s.at[k], dgz_r.at[e], (pe, t)))
    my_eight = pl.ds(pl.multiple_of(8 * (e // 8), 8), 8)
    dg_fin[pl.ds(e, 1)] = dg_mid[my_eight, :][None]

    arrived_panels(0)
    arrived_panels(1)

    def grams(index, source, is_left, meanwhile=lambda: None):
        lanes = stage_lanes(index)

        def product(first_row):
            if is_left:
                left_mt = mt[pl.ds(first_row, 1024), pl.ds(pl.multiple_of(group * 1024, 1024), 1024)]
                return jnp.dot(left_mt, source[...], preferred_element_type=F32)
            return jnp.dot(mt[pl.ds(first_row, 1024), :], source[...], preferred_element_type=F32)

        sib_out[:, lanes] = product(0).astype(BF16)
        swap = remote(
            sib_out.at[:, lanes],
            sib_in.at[:, lanes],
            sib_s.at[index],
            sib_r.at[index],
            (2 * z + 1 - c, t),
        )
        start(swap)
        own[:, lanes] = product(1024)
        result = meanwhile()
        swap.wait_recv()

        def block(steps):
            at = tile_rows(ring(steps))
            return own[at, lanes] + sib_in[at, lanes].astype(F32)

        if index == 2:
            for kind, steps in enumerate(DIRECT):
                z_out[kind, :, lanes] = block(steps).astype(BF16)
                start(z_copy(index, kind, steps))
            fin[:, lanes] = block(0)
            return result

        for kind, (target, to) in enumerate(((-4, -2), (-3, -1), (3, 1), (-1, -1), (1, 1))):
            z_out[kind, :, lanes] = block(target).astype(BF16)
            start(z_copy(index, kind, to))
        hold[0, :, lanes] = block(-2)
        hold[1, :, lanes] = block(2)
        fin[:, lanes] = block(0)
        return result

    def z_copy(index, kind, steps):
        lanes = stage_lanes(index)
        return remote(
            z_out.at[kind, :, lanes],
            z_in.at[kind, :, lanes],
            z_s.at[index, kind],
            z_r.at[index, kind],
            (2 * ring(steps) + c, t),
        )

    def relay(index):
        lanes = stage_lanes(index)
        z_copy(index, 0, 2).wait_recv()
        z_copy(index, 1, 1).wait_recv()
        far = z_in[0, :, lanes].astype(F32) + z_in[1, :, lanes].astype(F32)
        z_out[5, :, lanes] = (hold[0, :, lanes] + far).astype(BF16)
        start(z_copy(index, 5, -2))
        z_copy(index, 2, -1).wait_recv()
        z_out[6, :, lanes] = (hold[1, :, lanes] + z_in[2, :, lanes].astype(F32)).astype(BF16)
        start(z_copy(index, 6, 2))

    def gather_sum(index):
        lanes = stage_lanes(index)
        acc = fin[:, lanes]
        arriving = ((3, 1), (4, -1), (5, 2), (6, -2))
        if index == 2:
            arriving = [(kind, -steps) for kind, steps in enumerate(DIRECT)]
        for kind, steps in arriving:
            z_copy(index, kind, steps).wait_recv()
            acc = acc + z_in[kind, :, lanes].astype(F32)
        return acc.T * SCALE

    for k, pe in enumerate(experts):
        src = dg_mid.at[my_eight]
        remote(src, dg_fin.at[pe], dgz_s.at[k], dgz_r.at[pe], (pe, t)).wait_recv()
    eight = jnp.sum(dg_fin[...], axis=0)
    this = lax.broadcasted_iota(jnp.int32, (8, 128), 0) == e % 8
    dgram = jnp.sum(jnp.where(this, eight, 0.0), axis=0, keepdims=True) * SCALE
    colfac = jnp.sqrt(jnp.mean(dgram, axis=1, keepdims=True) / (dgram + 1e-05))
    grid_step = jnp.broadcast_to(colfac, (PANEL, PANEL)).T * step
    amp[...] = grid_step / (2.0 * math.pi)
    inv[...] = 1.0 / grid_step

    def round_columns(b):
        j0 = pl.multiple_of(b * 8, 8)
        at = pl.ds(j0, 8)
        rot[...] = pltpu.roll(ht[...], (PANEL - b * 8) % PANEL, 1)
        near = rot[at, :]
        block = work[at, :]
        inv_b, amp_b, dinv_b = inv[at, :], amp[at, :], dinv[at, :]
        row = lax.broadcasted_iota(jnp.int32, (8, 128), 0)
        faults = []
        fault_rows = jnp.zeros((8, 128), F32)
        for j in range(8):
            value = jnp.broadcast_to(block[j : j + 1], (8, 128))
            turns = value * jnp.broadcast_to(inv_b[j : j + 1], (8, 128))
            moved = sine_of_turns(turns) * jnp.broadcast_to(amp_b[j : j + 1], (8, 128))
            fault = moved * jnp.broadcast_to(dinv_b[j : j + 1], (8, 128))
            coef = jnp.broadcast_to(near[:, j : j + 1], (8, 128))
            block = jnp.where(row == j, value - moved, block - fault * coef)
            fault_rows = jnp.where(row == j, fault, fault_rows)
            faults.append(fault)
        for k in range(16):
            part = pl.ds(8 * k, 8)
            acc = work[part, :]
            for j in range(8):
                acc = acc - faults[j] * jnp.broadcast_to(rot[part, j : j + 1], (8, 128))
            work[part, :] = acc
        work[at, :] = block
        errs[at, :] = fault_rows

    @pl.loop(0, 16)
    def _(b):
        round_columns(b)

    def arrived_part(part):
        keeps[part].wait()
        for k, (py, px, pu) in enumerate(others):
            src = tokens.at[:, main_lanes(py, px, part)]
            dst = x_main[part].at[tile_rows(pu)]
            remote(src, dst, xm_s.at[part, k], xm_r.at[part, pu], (e, 4 * py + px)).wait_recv()

    arrived_panels(2)
    arrived_panels(3)

    send_part(1)

    for k, (py, px, pu) in enumerate(half_ring):
        if k == 0:
            keep_left.wait()
        else:
            src = tokens.at[:, left_lanes(py, px)]
            dst = x_left.at[tile_rows(pu - 8 * group)]
            remote(src, dst, xl_s.at[k], xl_r.at[pu - 8 * group], (e, 4 * py + px)).wait_recv()
    grams(0, x_left, True)


    err_rows = errs[...].T.astype(BF16)

    @pl.loop(0, 14)
    def _(i):
        lanes = pl.ds(pl.multiple_of(i * 512, 512), 512)
        fix = jnp.dot(err_rows, h_half[:, lanes], preferred_element_type=F32)
        updated[:, lanes] = (w_v[:, lanes].astype(F32) - fix).astype(BF16)

    updated[:, 0:PANEL] = work[...].T.astype(BF16)
    relay(0)

    arrived_part(0)
    def end_left():
        left[...] = gather_sum(0)
        half_rows = pl.ds(pl.multiple_of((1 - side) * 64, 64), 64)
        left_out[...] = left[half_rows, :]
        swap_left = remote(left_out, left_in, lx_s.at[0], lx_r.at[0], (e, 4 * y + x + 1 - 2 * side))
        start(swap_left)
        return swap_left

    swap_left = grams(1, x_two, False, end_left)

    arrived_part(1)
    grams(2, x_one, False, lambda: relay(1))

    base = 64 * side
    swap_left.wait_recv()
    left_at = pl.ds(pl.multiple_of(384 * (1 - side), 64), 64)
    gram[left_at, :] = left[pl.ds(pl.multiple_of(side * 64, 64), 64), :] + left_in[...]
    gram[pl.ds(pl.multiple_of(base, 64), 256), :] = gather_sum(1)
    gram[pl.ds(pl.multiple_of(base + 256, 64), 128), :] = gather_sum(2)

    for copy in sent:
        copy.wait_send()


def hand_over(gram_in, updated_in, gram, updated, sem):
    copies = [pltpu.make_async_copy(gram_in, gram, sem.at[8])]
    for i in range(8):
        at = pl.ds(16 * i, 16)
        copies.append(pltpu.make_async_copy(updated_in.at[at], updated.at[at], sem.at[i]))
    for copy in copies:
        copy.start()
    for copy in copies:
        copy.wait()


def body(tokens, routes, owner_of, weights, hinv_diag, hinv_rows):
    vmem = pl.BlockSpec(memory_space=pltpu.VMEM)
    hbm = pl.BlockSpec(memory_space=pl.ANY)
    dma = pltpu.SemaphoreType.DMA
    square = pltpu.VMEM((PANEL, PANEL), F32)
    gram, updated = pl.pallas_call(
        kernel,
        out_shape=(pltpu.VMEM((SHARE, PANEL), F32), pltpu.VMEM((128, D), BF16)),
        in_specs=[hbm] * 6,
        out_specs=(vmem, vmem),
        scratch_shapes=[
            pltpu.VMEM((TOP, TOK), jnp.int32),
            pltpu.SMEM((SLOTS,), jnp.int32),
            pltpu.VMEM((1, PANEL), F32),
            pltpu.VMEM((TOK, 128), BF16),
            pltpu.VMEM((PLANE, MSG, TOK), BF16),
            pltpu.VMEM((128, D), BF16),
            pltpu.VMEM((PANEL, D), F32),
            pltpu.VMEM((PANEL, D), BF16),
            pltpu.VMEM((SLOTS, PANEL), F32),
            pltpu.VMEM((PLANE, SLOTS, PANEL), F32),
            pltpu.VMEM((SLOTS, PANEL), F32),
            pltpu.VMEM((16, 8, PANEL), F32),
            pltpu.VMEM((SLOTS * PANEL, PLANE * TOK), BF16),
            pltpu.VMEM((8 * TOK, 128), BF16),
            pltpu.VMEM((PLANE * TOK, 256), BF16),
            pltpu.VMEM((PLANE * TOK, 128), BF16),
            square,
            square,
            square,
            square,
            square,
            square,
            square,
            pltpu.VMEM((RING * PANEL, 512), BF16),
            pltpu.VMEM((RING * PANEL, 512), BF16),
            pltpu.VMEM((RING * PANEL, 512), F32),
            pltpu.VMEM((7, PANEL, 512), BF16),
            pltpu.VMEM((7, PANEL, 512), BF16),
            pltpu.VMEM((2, PANEL, 512), F32),
            pltpu.VMEM((PANEL, 512), F32),
            square,
            pltpu.VMEM((64, PANEL), F32),
            pltpu.VMEM((64, PANEL), F32),
            dma((11,)),
            dma((15,)),
            dma((16,)),
            dma((15,)),
            dma((16,)),
            dma((16,)),
            dma((16,)),
            dma((4,)),
            dma((4,)),
            dma((8,)),
            dma((8,)),
            dma((2, 15)),
            dma((2, 16)),
            dma((3,)),
            dma((3,)),
            dma((3, 7)),
            dma((3, 7)),
            dma((1,)),
            dma((1,)),
        ],
        compiler_params=pltpu.CompilerParams(
            collective_id=0, has_side_effects=True, vmem_limit_bytes=61 * 2**20
        ),
        cost_estimate=pl.CostEstimate(flops=4 * 10**9, bytes_accessed=10**7, transcendentals=0),
        name="calibrate",
    )(tokens, routes.T, owner_of, weights[0], hinv_diag, hinv_rows[0])
    gram, updated = pl.pallas_call(
        hand_over,
        out_shape=(
            jax.ShapeDtypeStruct((SHARE, PANEL), F32),
            jax.ShapeDtypeStruct((128, D), BF16),
        ),
        in_specs=[vmem, vmem],
        out_specs=(hbm, hbm),
        scratch_shapes=[dma((9,))],
        name="hand_over",
    )(
        pltpu.with_memory_space_constraint(gram, pltpu.VMEM),
        pltpu.with_memory_space_constraint(updated, pltpu.VMEM),
    )
    return gram[None], updated[None]


def solution(mesh):
    in_specs = (
        P(("expert", "token"), None),
        P(("expert", "token"), None),
        P(),
        P("expert", "token", None),
        P("expert", None),
        P("expert", None, None),
    )
    out_specs = (P("expert", "token", None), P("expert", "token", None))
    return jax.shard_map(body, mesh=mesh, in_specs=in_specs, out_specs=out_specs, check_vma=False)
```

```python
import math

import jax
import jax.numpy as jnp
from jax import lax
from jax.experimental import pallas as pl
from jax.experimental.pallas import tpu as pltpu
from jax.sharding import PartitionSpec as P

D = 7168
PANEL = 128
TOP = 2
TOK = 128
SLOTS = 16
RING = 8
PLANE = 16
SHARE = 448
MSG = PANEL + SLOTS
MESH = pl.DeviceIdType.MESH
BF16 = jnp.bfloat16
F32 = jnp.float32
SCALE = 16.0 / 65536.0

SINE = (
    6.2831852700170625,
    -16.20895564378196,
    16.769189671870134,
    -9.624604702175908,
    3.5163760294927235,
    -0.7983429889808796,
)


def sine_of_turns(turns):
    r = turns - jnp.round(turns)
    y = r * r
    y2 = y * y
    low = SINE[0] + SINE[1] * y
    mid = SINE[2] + SINE[3] * y
    top = SINE[4] + SINE[5] * y
    edge = r - 4.0 * (r * y)
    return edge * (low + y2 * (mid + y2 * top))


DIRECT = (4, 3, -3, 2, -2, 1, -1)


def place_of(x):
    return jnp.where(x == 0, 0, jnp.where(x == 3, 1, x + 1))


def kernel(
    tokens,
    routes_in,
    owner_in,
    weights,
    hdiag_in,
    hrows,
    gram,
    updated,
    routes,
    owner,
    hdiag,
    x0,
    msg,
    w_v,
    h_v,
    h_half,
    dg_own,
    dg_in,
    dg_mid,
    dg_fin,
    mt,
    x_left,
    x_two,
    x_one,
    ht,
    rot,
    work,
    inv,
    amp,
    dinv,
    errs,
    sib_out,
    sib_in,
    own,
    z_out,
    z_in,
    hold,
    fin,
    left,
    left_out,
    left_in,
    local_sem,
    dg_s,
    dg_r,
    dgz_s,
    dgz_r,
    pm_s,
    pm_r,
    pc_s,
    pc_r,
    xl_s,
    xl_r,
    xm_s,
    xm_r,
    sib_s,
    sib_r,
    z_s,
    z_r,
    lx_s,
    lx_r,
):
    e = lax.axis_index("expert")
    t = lax.axis_index("token")
    z, c = e // 2, e % 2
    y, x = t // 4, t % 4
    place = place_of(x)
    u = 4 * place + y
    group = place // 2
    side = x % 2

    ys = [y] + [(y + k) % 4 for k in range(1, 4)]
    xs = [x, 3 - x, (x + 2) % 4, (5 - x) % 4]
    places = [place] + [place_of(px) for px in xs[1:]]
    plane = [(ys[k // 4], xs[k % 4], 4 * places[k % 4] + ys[k // 4]) for k in range(16)]
    others = plane[1:]
    half_ring = [plane[4 * (k // 2) + k % 2] for k in range(8)]
    experts = [(e + k) % 16 for k in range(1, 16)]

    def ring(steps):
        return (z + jnp.where(c == 0, steps % RING, -steps % RING)) % RING

    def tile_rows(index):
        return pl.ds(pl.multiple_of(index * TOK, TOK), TOK)

    def main_lanes(py, px, part):
        first = 7 * (2 * py + px // 2) + 4 * (px % 2) + 2 * part
        return pl.ds(pl.multiple_of(first * 128, 128), 256 - 128 * part)

    def stage_lanes(index):
        return (pl.ds(0, 128), pl.ds(128, 256), pl.ds(384, 128))[index]

    def left_lanes(py, px):
        return pl.ds(pl.multiple_of((7 * (2 * py + px // 2) + 3) * 128, 128), 128)

    def remote(src, dst, send, recv, device):
        return pltpu.make_async_remote_copy(
            src_ref=src,
            dst_ref=dst,
            send_sem=send,
            recv_sem=recv,
            device_id=device,
            device_id_type=MESH,
        )

    sent = []

    def start(copy):
        copy.start()
        sent.append(copy)

    barrier = pltpu.get_barrier_semaphore()
    for pe in experts:
        pl.semaphore_signal(barrier, inc=1, device_id=(pe, t), device_id_type=MESH)
    for py, px, _ in others:
        pl.semaphore_signal(barrier, inc=1, device_id=(e, 4 * py + px), device_id_type=MESH)

    get_x0 = pltpu.make_async_copy(tokens.at[:, pl.ds(0, 128)], x0, local_sem.at[0])
    get_w = pltpu.make_async_copy(weights, w_v, local_sem.at[1])
    get_h = pltpu.make_async_copy(hrows, h_v, local_sem.at[2])
    get_small = [
        pltpu.make_async_copy(routes_in, routes, local_sem.at[8]),
        pltpu.make_async_copy(owner_in, owner, local_sem.at[9]),
        pltpu.make_async_copy(hdiag_in, hdiag, local_sem.at[10]),
    ]
    for copy in get_small:
        copy.start()
    get_x0.start()
    get_w.start()
    get_h.start()

    for copy in get_small:
        copy.wait()
    first = jnp.broadcast_to(routes[0:1, :], (SLOTS, TOK))
    second = jnp.broadcast_to(routes[1:2, :], (SLOTS, TOK))
    slot_a = jnp.zeros((SLOTS, TOK), jnp.int32)
    slot_b = jnp.zeros((SLOTS, TOK), jnp.int32)
    for i in range(SLOTS):
        slot_a = jnp.where(first == i, owner[i], slot_a)
        slot_b = jnp.where(second == i, owner[i], slot_b)
    slot_row = lax.broadcasted_iota(jnp.int32, (SLOTS, TOK), 0)
    mask = jnp.where((slot_a == slot_row) | (slot_b == slot_row), 1.0, 0.0).astype(F32)

    get_x0.wait()
    panel = x0[...].astype(F32)
    square = panel * panel
    high = square.astype(BF16)
    low = (square - high.astype(F32)).astype(BF16)
    mask16 = mask.astype(BF16)
    dg_own[...] = jnp.dot(mask16, high, preferred_element_type=F32) + jnp.dot(
        mask16, low, preferred_element_type=F32
    )
    msg[pl.ds(u, 1), pl.ds(0, PANEL), :] = panel.T.astype(BF16)[None]
    msg[pl.ds(u, 1), pl.ds(PANEL, SLOTS), :] = mask16[None]

    pl.semaphore_wait(barrier, 30)

    for k, (py, px, _) in enumerate(others):
        start(remote(dg_own, dg_in.at[u], dg_s.at[k], dg_r.at[u], (e, 4 * py + px)))
    for k in range(1, 8):
        py, px, _ = half_ring[k]
        start(remote(msg.at[u], msg.at[u], pm_s.at[k], pm_r.at[u], (e, 4 * py + px)))
    for k, (py, px, _) in enumerate(half_ring):
        src = tokens.at[:, left_lanes(py, px)]
        dst = x_left.at[tile_rows(u - 8 * group)]
        if k == 0:
            keep_left = pltpu.make_async_copy(src, dst, local_sem.at[3])
            keep_left.start()
        else:
            start(remote(src, dst, xl_s.at[k], xl_r.at[u - 8 * group], (e, 4 * py + px)))

    x_main = (x_two, x_one)
    keeps = []
    for part in range(2):
        keep = pltpu.make_async_copy(
            tokens.at[:, main_lanes(y, x, part)], x_main[part].at[tile_rows(u)], local_sem.at[4 + part]
        )
        keep.start()
        keeps.append(keep)
    dg_in[pl.ds(u, 1)] = dg_own[...][None]

    for k in range(1, 4):
        pu = 4 * place + ys[k]
        remote(msg.at[pu], msg.at[pu], pm_s.at[0], pm_r.at[pu], (e, 4 * ys[k] + x)).wait_recv()
    column = pl.ds(4 * place, 4)
    for k in (2, 3):
        start(remote(msg.at[column], msg.at[column], pc_s.at[k], pc_r.at[x], (e, 4 * y + xs[k])))
    def send_part(part):
        for k, (py, px, _) in enumerate(others):
            src = tokens.at[:, main_lanes(py, px, part)]
            dst = x_main[part].at[tile_rows(u)]
            start(remote(src, dst, xm_s.at[part, k], xm_r.at[part, u], (e, 4 * py + px)))

    send_part(0)

    get_w.wait()
    get_h.wait()
    wide = w_v[:, 0:PANEL].astype(F32).T
    work[...] = wide
    step = jnp.max(jnp.abs(wide), axis=0, keepdims=True) / 7.0 + 1e-06
    cols = lax.broadcasted_iota(jnp.int32, (PANEL, PANEL), 0)
    rows = lax.broadcasted_iota(jnp.int32, (PANEL, PANEL), 1)
    ht[...] = jnp.where(cols > rows, h_v[:, 0:PANEL].T, 0.0)
    dinv[...] = 1.0 / jnp.broadcast_to(hdiag[...], (PANEL, PANEL)).T

    @pl.loop(0, 14)
    def _(i):
        lanes = pl.ds(pl.multiple_of(i * 512, 512), 512)
        h_half[:, lanes] = h_v[:, lanes].astype(BF16)


    def mask_panel(sender):
        their = msg[sender, 0:PANEL, :]
        flags = msg[sender, PANEL:MSG, :]
        lanes = tile_rows(sender)
        for s in range(SLOTS):
            value = their * jnp.broadcast_to(flags[s : s + 1], (PANEL, TOK))
            at = jnp.where(c == s % 2, 1024, 0) + (s // 2) * PANEL
            mt[pl.ds(pl.multiple_of(at, PANEL), PANEL), lanes] = value

    def arrived_panels(column):
        if column == 1:
            for k in range(4):
                pu = 4 * places[1] + ys[k]
                remote(msg.at[pu], msg.at[pu], pm_s.at[0], pm_r.at[pu], (e, 4 * ys[k] + xs[1])).wait_recv()
        if column > 1:
            theirs = pl.ds(4 * places[column], 4)
            px = xs[column]
            remote(msg.at[theirs], msg.at[theirs], pc_s.at[column], pc_r.at[px], (e, 4 * y + px)).wait_recv()

        @pl.loop(0, 4)
        def _(i):
            mask_panel(4 * places[column] + i)

    for k, (py, px, pu) in enumerate(others):
        remote(dg_own, dg_in.at[pu], dg_s.at[k], dg_r.at[pu], (e, 4 * py + px)).wait_recv()
    dg_mid[...] = jnp.sum(dg_in[...], axis=0)
    for k, pe in enumerate(experts):
        src = dg_mid.at[pl.ds(pl.multiple_of(8 * (pe // 8), 8), 8)]
        start(remote(src, dg_fin.at[e], dgz_s.at[k], dgz_r.at[e], (pe, t)))
    my_eight = pl.ds(pl.multiple_of(8 * (e // 8), 8), 8)
    dg_fin[pl.ds(e, 1)] = dg_mid[my_eight, :][None]

    arrived_panels(0)
    arrived_panels(1)

    def grams(index, source, is_left, meanwhile=lambda: None):
        lanes = stage_lanes(index)

        def product(first_row):
            if is_left:
                left_mt = mt[pl.ds(first_row, 1024), pl.ds(pl.multiple_of(group * 1024, 1024), 1024)]
                return jnp.dot(left_mt, source[...], preferred_element_type=F32)
            return jnp.dot(mt[pl.ds(first_row, 1024), :], source[...], preferred_element_type=F32)

        sib_out[:, lanes] = product(0).astype(BF16)
        swap = remote(
            sib_out.at[:, lanes],
            sib_in.at[:, lanes],
            sib_s.at[index],
            sib_r.at[index],
            (2 * z + 1 - c, t),
        )
        start(swap)
        own[:, lanes] = product(1024)
        result = meanwhile()
        swap.wait_recv()

        def block(steps):
            at = tile_rows(ring(steps))
            return own[at, lanes] + sib_in[at, lanes].astype(F32)

        if index == 2:
            for kind, steps in enumerate(DIRECT):
                z_out[kind, :, lanes] = block(steps).astype(BF16)
                start(z_copy(index, kind, steps))
            fin[:, lanes] = block(0)
            return result

        for kind, (target, to) in enumerate(((-4, -2), (-3, -1), (3, 1), (-1, -1), (1, 1))):
            z_out[kind, :, lanes] = block(target).astype(BF16)
            start(z_copy(index, kind, to))
        hold[0, :, lanes] = block(-2)
        hold[1, :, lanes] = block(2)
        fin[:, lanes] = block(0)
        return result

    def z_copy(index, kind, steps):
        lanes = stage_lanes(index)
        return remote(
            z_out.at[kind, :, lanes],
            z_in.at[kind, :, lanes],
            z_s.at[index, kind],
            z_r.at[index, kind],
            (2 * ring(steps) + c, t),
        )

    def relay(index):
        lanes = stage_lanes(index)
        z_copy(index, 0, 2).wait_recv()
        z_copy(index, 1, 1).wait_recv()
        far = z_in[0, :, lanes].astype(F32) + z_in[1, :, lanes].astype(F32)
        z_out[5, :, lanes] = (hold[0, :, lanes] + far).astype(BF16)
        start(z_copy(index, 5, -2))
        z_copy(index, 2, -1).wait_recv()
        z_out[6, :, lanes] = (hold[1, :, lanes] + z_in[2, :, lanes].astype(F32)).astype(BF16)
        start(z_copy(index, 6, 2))

    def gather_sum(index):
        lanes = stage_lanes(index)
        acc = fin[:, lanes]
        arriving = ((3, 1), (4, -1), (5, 2), (6, -2))
        if index == 2:
            arriving = [(kind, -steps) for kind, steps in enumerate(DIRECT)]
        for kind, steps in arriving:
            z_copy(index, kind, steps).wait_recv()
            acc = acc + z_in[kind, :, lanes].astype(F32)
        return acc.T * SCALE

    for k, pe in enumerate(experts):
        src = dg_mid.at[my_eight]
        remote(src, dg_fin.at[pe], dgz_s.at[k], dgz_r.at[pe], (pe, t)).wait_recv()
    eight = jnp.sum(dg_fin[...], axis=0)
    this = lax.broadcasted_iota(jnp.int32, (8, 128), 0) == e % 8
    dgram = jnp.sum(jnp.where(this, eight, 0.0), axis=0, keepdims=True) * SCALE
    colfac = jnp.sqrt(jnp.mean(dgram, axis=1, keepdims=True) / (dgram + 1e-05))
    grid_step = jnp.broadcast_to(colfac, (PANEL, PANEL)).T * step
    amp[...] = grid_step / (2.0 * math.pi)
    inv[...] = 1.0 / grid_step

    def round_columns(b, first):
        j0 = pl.multiple_of(b * 8, 8)
        at = pl.ds(j0, 8)
        rot[...] = pltpu.roll(ht[...], (PANEL - b * 8) % PANEL, 1)
        near = rot[at, :]
        block = work[at, :]
        inv_b, amp_b, dinv_b = inv[at, :], amp[at, :], dinv[at, :]
        row = lax.broadcasted_iota(jnp.int32, (8, 128), 0)
        faults = []
        fault_rows = jnp.zeros((8, 128), F32)
        for j in range(8):
            value = jnp.broadcast_to(block[j : j + 1], (8, 128))
            turns = value * jnp.broadcast_to(inv_b[j : j + 1], (8, 128))
            moved = sine_of_turns(turns) * jnp.broadcast_to(amp_b[j : j + 1], (8, 128))
            fault = moved * jnp.broadcast_to(dinv_b[j : j + 1], (8, 128))
            coef = jnp.broadcast_to(near[:, j : j + 1], (8, 128))
            block = jnp.where(row == j, value - moved, block - fault * coef)
            fault_rows = jnp.where(row == j, fault, fault_rows)
            faults.append(fault)

        def pass_on(k):
            part = pl.ds(8 * k, 8)
            acc = work[part, :]
            for j in range(8):
                acc = acc - faults[j] * jnp.broadcast_to(rot[part, j : j + 1], (8, 128))
            work[part, :] = acc

        for k in range(first, 16):
            pass_on(k)
        work[at, :] = block
        errs[at, :] = fault_rows

    for quarter in range(4):

        @pl.loop(4 * quarter, 4 * quarter + 4)
        def _(b):
            round_columns(b, 4 * quarter)

    def arrived_part(part):
        keeps[part].wait()
        for k, (py, px, pu) in enumerate(others):
            src = tokens.at[:, main_lanes(py, px, part)]
            dst = x_main[part].at[tile_rows(pu)]
            remote(src, dst, xm_s.at[part, k], xm_r.at[part, pu], (e, 4 * py + px)).wait_recv()

    arrived_panels(2)
    arrived_panels(3)

    send_part(1)

    for k, (py, px, pu) in enumerate(half_ring):
        if k == 0:
            keep_left.wait()
        else:
            src = tokens.at[:, left_lanes(py, px)]
            dst = x_left.at[tile_rows(pu - 8 * group)]
            remote(src, dst, xl_s.at[k], xl_r.at[pu - 8 * group], (e, 4 * py + px)).wait_recv()
    grams(0, x_left, True)


    err_rows = errs[...].T.astype(BF16)

    @pl.loop(0, 14)
    def _(i):
        lanes = pl.ds(pl.multiple_of(i * 512, 512), 512)
        fix = jnp.dot(err_rows, h_half[:, lanes], preferred_element_type=F32)
        updated[:, lanes] = (w_v[:, lanes].astype(F32) - fix).astype(BF16)

    updated[:, 0:PANEL] = work[...].T.astype(BF16)
    relay(0)

    arrived_part(0)
    def end_left():
        left[...] = gather_sum(0)
        half_rows = pl.ds(pl.multiple_of((1 - side) * 64, 64), 64)
        left_out[...] = left[half_rows, :]
        swap_left = remote(left_out, left_in, lx_s.at[0], lx_r.at[0], (e, 4 * y + x + 1 - 2 * side))
        start(swap_left)
        return swap_left

    swap_left = grams(1, x_two, False, end_left)

    arrived_part(1)
    grams(2, x_one, False, lambda: relay(1))

    base = 64 * side
    swap_left.wait_recv()
    left_at = pl.ds(pl.multiple_of(384 * (1 - side), 64), 64)
    gram[left_at, :] = left[pl.ds(pl.multiple_of(side * 64, 64), 64), :] + left_in[...]
    gram[pl.ds(pl.multiple_of(base, 64), 256), :] = gather_sum(1)
    gram[pl.ds(pl.multiple_of(base + 256, 64), 128), :] = gather_sum(2)

    for copy in sent:
        copy.wait_send()


def hand_over(gram_in, updated_in, gram, updated, sem):
    copies = [pltpu.make_async_copy(gram_in, gram, sem.at[8])]
    for i in range(8):
        at = pl.ds(16 * i, 16)
        copies.append(pltpu.make_async_copy(updated_in.at[at], updated.at[at], sem.at[i]))
    for copy in copies:
        copy.start()
    for copy in copies:
        copy.wait()


def body(tokens, routes, owner_of, weights, hinv_diag, hinv_rows):
    vmem = pl.BlockSpec(memory_space=pltpu.VMEM)
    hbm = pl.BlockSpec(memory_space=pl.ANY)
    dma = pltpu.SemaphoreType.DMA
    square = pltpu.VMEM((PANEL, PANEL), F32)
    gram, updated = pl.pallas_call(
        kernel,
        out_shape=(pltpu.VMEM((SHARE, PANEL), F32), pltpu.VMEM((128, D), BF16)),
        in_specs=[hbm] * 6,
        out_specs=(vmem, vmem),
        scratch_shapes=[
            pltpu.VMEM((TOP, TOK), jnp.int32),
            pltpu.SMEM((SLOTS,), jnp.int32),
            pltpu.VMEM((1, PANEL), F32),
            pltpu.VMEM((TOK, 128), BF16),
            pltpu.VMEM((PLANE, MSG, TOK), BF16),
            pltpu.VMEM((128, D), BF16),
            pltpu.VMEM((PANEL, D), F32),
            pltpu.VMEM((PANEL, D), BF16),
            pltpu.VMEM((SLOTS, PANEL), F32),
            pltpu.VMEM((PLANE, SLOTS, PANEL), F32),
            pltpu.VMEM((SLOTS, PANEL), F32),
            pltpu.VMEM((16, 8, PANEL), F32),
            pltpu.VMEM((SLOTS * PANEL, PLANE * TOK), BF16),
            pltpu.VMEM((8 * TOK, 128), BF16),
            pltpu.VMEM((PLANE * TOK, 256), BF16),
            pltpu.VMEM((PLANE * TOK, 128), BF16),
            square,
            square,
            square,
            square,
            square,
            square,
            square,
            pltpu.VMEM((RING * PANEL, 512), BF16),
            pltpu.VMEM((RING * PANEL, 512), BF16),
            pltpu.VMEM((RING * PANEL, 512), F32),
            pltpu.VMEM((7, PANEL, 512), BF16),
            pltpu.VMEM((7, PANEL, 512), BF16),
            pltpu.VMEM((2, PANEL, 512), F32),
            pltpu.VMEM((PANEL, 512), F32),
            square,
            pltpu.VMEM((64, PANEL), F32),
            pltpu.VMEM((64, PANEL), F32),
            dma((11,)),
            dma((15,)),
            dma((16,)),
            dma((15,)),
            dma((16,)),
            dma((16,)),
            dma((16,)),
            dma((4,)),
            dma((4,)),
            dma((8,)),
            dma((8,)),
            dma((2, 15)),
            dma((2, 16)),
            dma((3,)),
            dma((3,)),
            dma((3, 7)),
            dma((3, 7)),
            dma((1,)),
            dma((1,)),
        ],
        compiler_params=pltpu.CompilerParams(
            collective_id=0, has_side_effects=True, vmem_limit_bytes=61 * 2**20
        ),
        cost_estimate=pl.CostEstimate(flops=4 * 10**9, bytes_accessed=10**7, transcendentals=0),
        name="calibrate",
    )(tokens, routes.T, owner_of, weights[0], hinv_diag, hinv_rows[0])
    gram, updated = pl.pallas_call(
        hand_over,
        out_shape=(
            jax.ShapeDtypeStruct((SHARE, PANEL), F32),
            jax.ShapeDtypeStruct((128, D), BF16),
        ),
        in_specs=[vmem, vmem],
        out_specs=(hbm, hbm),
        scratch_shapes=[dma((9,))],
        name="hand_over",
    )(
        pltpu.with_memory_space_constraint(gram, pltpu.VMEM),
        pltpu.with_memory_space_constraint(updated, pltpu.VMEM),
    )
    return gram[None], updated[None]


def solution(mesh):
    in_specs = (
        P(("expert", "token"), None),
        P(("expert", "token"), None),
        P(),
        P("expert", "token", None),
        P("expert", None),
        P("expert", None, None),
    )
    out_specs = (P("expert", "token", None), P("expert", "token", None))
    return jax.shard_map(body, mesh=mesh, in_specs=in_specs, out_specs=out_specs, check_vma=False)
```
